32 devices in a mesh: rep: 2 (over y), ep: 16 (over z, x, core).
Axes of the slice: x: 2, y: 2, z: 4, core: 2. Of those that a mesh axis runs over, the one named last changes fastest.
Arguments:
- tokens: bfloat16 [4096, 2048], P(('rep', 'ep')), may hold values from -6 to 6
- expert_ids: int32 [4096, 6], P(('rep', 'ep')), may hold values from 0 to 15, all different within a row; in each aligned block of 128 rows (0 to 127, 128 to 255, ...) at most 64 rows name the same one
- gate_weights: float32 [4096, 6], P(('rep', 'ep')), may hold values from 0.03 to 0.5
- cotangent: bfloat16 [4096, 2048], P(('rep', 'ep')), may hold values from -4 to 4
- w_gate: bfloat16 [16, 2048, 704], P('ep'), may hold values from -0.125 to 0.125
- w_up: bfloat16 [16, 2048, 704], P('ep'), may hold values from -0.125 to 0.125
- w_down: bfloat16 [16, 704, 2048], P('ep'), may hold values from -0.21875 to 0.21875
Outputs:
- mixed: bfloat16 [4096, 2048], P(('rep', 'ep'))
- token_grad: bfloat16 [4096, 2048], P(('rep', 'ep'))
- gate_grad: float32 [4096, 6], P(('rep', 'ep'))
- grad_w_gate: float32 [16, 2048, 704], P('ep', 'rep')
- grad_w_up: float32 [16, 2048, 704], P('ep', 'rep')
- grad_w_down: float32 [16, 704, 2048], P('ep', 'rep')
The draws below stay inside these ranges and needn't reach their ends.
Inputs may be any that keep to these rules, and one draw needn't show every extreme that they name: `expert_ids`: A token's 6 expert ids are distinct; among the tokens of one device no expert is named by more than 64 choices.
All inputs are finite; a program needn't handle non-finite values.
Results may differ from the reference program's by a relative error of at most 0.0085.
Values may be sent and summed in bfloat16 or wider, within the bound.
A program may use at most 128 MiB of HBM per device.

```python
import math
import jax
import jax.numpy as jnp
import numpy as np
from jax import lax

D = 2048
TOP = 6
FF = 704
TOK_DEV = 128
EXPERTS = 16
CAP = 64
TOKENS = 4096
N_REP = 2
N_EP = 16


def block_scale(key, dims, split, smallest, top_value):
    def one(axis_at, shards_of):
        heights = jax.random.uniform(jax.random.fold_in(jax.random.fold_in(key, 6), axis_at), (shards_of,), jnp.float32, smallest / len(split), top_value / len(split))
        return jnp.repeat(jnp.exp(heights), dims[axis_at] // shards_of).reshape((-1,) + (1,) * (len(dims) - axis_at - 1))

    level = one(*split[0])
    for cut in split[1:]:
        level = level * one(*cut)
    return level


def shared_out(key, own, number, rows, amount, top, limit, lean):
    ranking = jax.random.permutation(key, amount)
    crowded, usual = shares(amount, rows * top, limit, lean, True), shares(amount, rows * top, limit, lean, False)
    places = jnp.arange(amount)

    def named(sizes, offset_by):
        used = int((sizes > 0).sum())
        fixed = max(1, used // 4)
        passed = fixed + (places - fixed + offset_by * (used - fixed)) % max(1, amount - fixed)
        return jnp.zeros((amount,), jnp.int32).at[ranking[jnp.where(places < fixed, places, passed)]].set(jnp.asarray(sizes, jnp.int32))

    sizes = jnp.where(number % 4 == 0, named(crowded, number // 4), named(usual, number - number // 4 - 1))
    mixed = jax.random.permutation(jax.random.fold_in(own, 3), amount)
    giver, receiver = mixed[0:amount // 2 * 2:2], mixed[1:amount // 2 * 2:2]
    margin = jnp.minimum(sizes[giver] - 1, limit - sizes[receiver]) // 2
    margin = jnp.where((giver == ranking[0]) | (receiver == ranking[0]) | (sizes[receiver] == 0), 0, jnp.maximum(margin, 0))
    passed = jax.random.randint(jax.random.fold_in(own, 4), (amount // 2,), 0, 1 << 20) % (margin + 1)
    sizes = sizes.at[giver].add(-passed).at[receiver].add(passed)
    labels = jnp.searchsorted(jnp.cumsum(sizes), jnp.arange(rows * top), side="right").astype(jnp.int32)
    grid = labels.reshape(top, rows).T
    grid = grid[jax.random.permutation(jax.random.fold_in(own, 1), rows)]
    offset_by = jax.random.randint(jax.random.fold_in(own, 2), (rows, 1), 0, top)
    return jnp.take_along_axis(grid, (jnp.arange(top)[None, :] + offset_by) % top, axis=1)


def shares(count, total, limit, skew, full):
    loads = [(1 << 20) // math.isqrt(rank ** skew) + 1 for rank in range(1, count + 1)]
    largest = limit if full else min(limit, max(-(-total // count), total * loads[0] // sum(loads)))
    least = 1 if total - largest >= count - 1 else 0
    given, spare = [largest] + [least] * (count - 1), total - largest - least * (count - 1)
    while spare > 0:
        movable = [i for i in range(1, count) if given[i] < largest] or [i for i in range(1, count) if given[i] < limit]
        whole, remaining = sum([loads[i] for i in movable]), spare
        for i in movable:
            extra = min(limit - given[i], max(1, remaining * loads[i] // whole), spare)
            given[i] = given[i] + extra
            spare = spare - extra
    return np.array(given)


def centred(rng, extent, deviation, most, pieces=(), kind=jnp.bfloat16):
    array = jax.random.normal(rng, extent, jnp.float32) * deviation
    if len(pieces) > 0:
        array = block_scale(rng, extent, pieces, -0.22, 0.18) * array
    return jnp.clip(array, min=-most, max=most).astype(kind)


def setup_inputs(seed: int = 0) -> dict:
    seeds = jax.random.split(jax.random.key(seed), 8)
    tokens = centred(seeds[0], (TOKENS, D), 1.0, 6.0, ((0, 32),))
    expert_ids_keys = jax.random.split(jax.random.fold_in(seeds[1], 1), TOKENS // TOK_DEV)
    expert_ids_turns = jax.random.permutation(jax.random.fold_in(seeds[1], 3), TOKENS // TOK_DEV)
    expert_ids = jax.vmap(lambda own, number: shared_out(jax.random.fold_in(seeds[1], 2), own, number, TOK_DEV, EXPERTS, TOP, CAP, 2))(expert_ids_keys, expert_ids_turns).reshape((TOKENS, TOP))
    gate_weights = jnp.clip(jnp.exp(math.log(0.5) - 2.8134107 * jax.random.uniform(seeds[2], (TOKENS, TOP), jnp.float32) ** block_scale(seeds[2], (TOKENS, TOP), ((0, 32),), -0.2, 0.2)), 0.03, 0.5)
    cotangent = centred(seeds[3], (TOKENS, D), 0.5, 4.0, ((0, 32),))
    w_gate = centred(seeds[4], (EXPERTS, D, FF), D ** -0.5, 0.125, ((0, 16),))
    w_up = centred(seeds[5], (EXPERTS, D, FF), D ** -0.5, 0.125, ((0, 16),))
    w_down = centred(seeds[6], (EXPERTS, FF, D), FF ** -0.5, 0.21875, ((0, 16),))
    return dict(tokens=tokens, expert_ids=expert_ids, gate_weights=gate_weights, cotangent=cotangent, w_gate=w_gate, w_up=w_up, w_down=w_down)


def expert_pass(args):
    rows, d_rows, gate_matrix, up_matrix, down_matrix = args
    gate_pre = jnp.dot(rows, gate_matrix, preferred_element_type=jnp.float32)
    up_pre = jnp.dot(rows, up_matrix, preferred_element_type=jnp.float32)
    sigmoid_val = jax.nn.sigmoid(gate_pre)
    silu_val = gate_pre * sigmoid_val
    act = (silu_val * up_pre).astype(jnp.bfloat16)
    expert_out = jnp.dot(act, down_matrix, preferred_element_type=jnp.float32).astype(jnp.bfloat16)
    act_grad = jnp.dot(d_rows, down_matrix.T, preferred_element_type=jnp.float32)
    gate_pre_grad = (act_grad * up_pre * sigmoid_val * (1.0 + gate_pre * (1.0 - sigmoid_val))).astype(jnp.bfloat16)
    up_pre_grad = (act_grad * silu_val).astype(jnp.bfloat16)
    row_grad = (jnp.dot(gate_pre_grad, gate_matrix.T, preferred_element_type=jnp.float32)
                + jnp.dot(up_pre_grad, up_matrix.T, preferred_element_type=jnp.float32)).astype(jnp.bfloat16)
    part_gate = jnp.dot(rows.T, gate_pre_grad, preferred_element_type=jnp.float32)
    part_up = jnp.dot(rows.T, up_pre_grad, preferred_element_type=jnp.float32)
    part_down = jnp.dot(act.T, d_rows, preferred_element_type=jnp.float32)
    return expert_out, row_grad, part_gate, part_up, part_down


def rounded(value):
    return lax.optimization_barrier(value.astype(jnp.bfloat16)).astype(jnp.float32)


def block_slots(ids_block):
    flat_ids = ids_block.reshape(N_EP, TOK_DEV * TOP)
    onehot = (flat_ids[:, :, None] == jnp.arange(EXPERTS, dtype=jnp.int32)[None, None, :]).astype(jnp.int32)
    before = jnp.cumsum(onehot, axis=1) - onehot
    return jnp.sum(before * onehot, axis=2).reshape(N_EP * TOK_DEV, TOP).astype(jnp.int32)


def reference(tokens, expert_ids, gate_weights, cotangent, w_gate, w_up, w_down):
    group_size = N_EP * TOK_DEV
    pair_count = group_size * TOP
    sum_gate = jnp.zeros((EXPERTS, D, FF), jnp.float32)
    sum_up = jnp.zeros((EXPERTS, D, FF), jnp.float32)
    sum_down = jnp.zeros((EXPERTS, FF, D), jnp.float32)
    mixed_parts = []
    token_parts = []
    gate_parts = []
    for group in range(N_REP):
        low = group * group_size
        high = low + group_size
        tok_block = tokens[low:high]
        ids_block = expert_ids[low:high]
        slot_block = block_slots(ids_block)
        weight_block = gate_weights[low:high]
        cot_block = cotangent[low:high]
        source = (jnp.arange(group_size, dtype=jnp.int32) // TOK_DEV)[:, None]
        slot_index = ((ids_block * N_EP + source) * CAP + slot_block).reshape(-1).astype(jnp.int32)
        slot_owner = jnp.full((EXPERTS * N_EP * CAP,), pair_count, jnp.int32)
        slot_owner = slot_owner.at[slot_index].set(jnp.arange(pair_count, dtype=jnp.int32))
        padded_tokens = jnp.concatenate([tok_block, jnp.zeros((1, D), tok_block.dtype)], axis=0)
        dispatched = padded_tokens[slot_owner // TOP].reshape(EXPERTS, N_EP * CAP, D)
        scaled = (weight_block[:, :, None] * cot_block[:, None, :].astype(jnp.float32)).astype(jnp.bfloat16)
        scaled = jnp.concatenate([scaled.reshape(pair_count, D), jnp.zeros((1, D), scaled.dtype)], axis=0)
        scaled_cot = scaled[slot_owner].reshape(EXPERTS, N_EP * CAP, D)
        outs, row_grads, part_gate, part_up, part_down = lax.map(
            expert_pass, (dispatched, scaled_cot, w_gate, w_up, w_down))
        sum_gate = sum_gate + rounded(part_gate)
        sum_up = sum_up + rounded(part_up)
        sum_down = sum_down + rounded(part_down)
        picked = outs.reshape(-1, D)[slot_index].reshape(group_size, TOP, D).astype(jnp.float32)
        mixed_parts.append(jnp.sum(weight_block[:, :, None] * picked, axis=1).astype(jnp.bfloat16))
        gate_parts.append(jnp.sum(cot_block[:, None, :].astype(jnp.float32) * picked, axis=2))
        back_rows = row_grads.reshape(-1, D)[slot_index].reshape(group_size, TOP, D).astype(jnp.float32)
        token_parts.append(jnp.sum(back_rows, axis=1).astype(jnp.bfloat16))
    mixed = jnp.concatenate(mixed_parts, axis=0)
    token_grad = jnp.concatenate(token_parts, axis=0)
    gate_grad = jnp.concatenate(gate_parts, axis=0)
    return mixed, token_grad, gate_grad, sum_gate, sum_up, sum_down
```

```python
import jax
import jax.numpy as jnp
from jax import lax
from jax.sharding import PartitionSpec as P


def matmul(left, right, left_dim, right_dim):
    return lax.dot_general(
        left, right, (((left_dim,), (right_dim,)), ((), ())), preferred_element_type=jnp.float32
    )


def per_device(tokens, expert_ids, gate_weights, cotangent, w_gate, w_up, w_down):
    tok_rows, row_width = tokens.shape
    top_count = expert_ids.shape[1]
    expert_count = lax.axis_size("ep")
    capacity = top_count * tok_rows * 4 // (3 * expert_count)
    rows = expert_count * capacity
    gate_matrix = w_gate[0]
    up_matrix = w_up[0]
    down_matrix = w_down[0]

    chosen = expert_ids[:, :, None] == jnp.arange(expert_count, dtype=jnp.int32)[None, None, :]
    weights = jnp.sum(jnp.where(chosen, gate_weights[:, :, None], 0.0), axis=1)
    mine = lax.all_to_all(weights.T, "ep", split_axis=0, concat_axis=0, tiled=True)

    all_tokens = lax.all_gather(tokens, "ep", axis=0, tiled=True)
    all_cot = lax.all_gather(cotangent, "ep", axis=0, tiled=True)

    named = mine > 0.0
    before = jnp.cumsum(named.astype(jnp.int32), axis=1) - 1
    slot = jnp.where(named, before, -1)
    pick = slot[:, None, :] == jnp.arange(capacity, dtype=jnp.int32)[None, :, None]
    pick_b = pick.astype(jnp.bfloat16)
    gate = jnp.sum(jnp.where(pick, mine[:, None, :], 0.0), axis=2).reshape(rows, 1)

    def dispatch(everything):
        blocks = everything.reshape(expert_count, tok_rows, row_width)
        return (
            jnp.einsum("sct,std->scd", pick_b, blocks, preferred_element_type=jnp.float32)
            .astype(jnp.bfloat16)
            .reshape(rows, row_width)
        )

    def collect(part):
        part = part.astype(jnp.bfloat16).reshape(expert_count, capacity, row_width)
        spread = jnp.einsum("sct,scd->std", pick_b, part, preferred_element_type=jnp.float32)
        return lax.psum_scatter(
            spread.astype(jnp.bfloat16).reshape(expert_count * tok_rows, row_width),
            "ep",
            scatter_dimension=0,
            tiled=True,
        )

    def over_rep(part):
        return lax.psum_scatter(
            part.astype(jnp.bfloat16)[None], "rep", scatter_dimension=1, tiled=True
        ).astype(jnp.float32)

    x_rows = dispatch(all_tokens)
    gate_pre = matmul(x_rows, gate_matrix, 1, 0)
    up_pre = matmul(x_rows, up_matrix, 1, 0)
    sigmoid_val = jax.nn.sigmoid(gate_pre)
    silu_val = gate_pre * sigmoid_val
    act = silu_val * up_pre
    weighted = (gate * act).astype(jnp.bfloat16)
    mixed = collect(matmul(weighted, down_matrix, 1, 0))

    c_rows = dispatch(all_cot)
    grad_down = over_rep(matmul(weighted, c_rows, 0, 0))
    back = matmul(c_rows, down_matrix, 1, 1)
    act_grad = gate * back
    gate_pre_grad = (
        act_grad * up_pre * sigmoid_val * (1.0 + gate_pre * (1.0 - sigmoid_val))
    ).astype(jnp.bfloat16)
    up_pre_grad = (act_grad * silu_val).astype(jnp.bfloat16)
    pair_grad = jnp.sum(act * back, axis=1).reshape(expert_count, capacity, 1)
    row_grad = matmul(gate_pre_grad, gate_matrix, 1, 1) + matmul(up_pre_grad, up_matrix, 1, 1)
    token_grad = collect(row_grad)
    grad_gate = over_rep(matmul(x_rows, gate_pre_grad, 0, 0))
    grad_up = over_rep(matmul(x_rows, up_pre_grad, 0, 0))

    token_pair = jnp.sum(jnp.where(pick, pair_grad, 0.0), axis=1)
    pairs = lax.all_to_all(token_pair, "ep", split_axis=0, concat_axis=0, tiled=True)
    gate_grad = jnp.sum(jnp.where(chosen, pairs.T[:, None, :], 0.0), axis=2)
    return (mixed, token_grad, gate_grad, grad_gate, grad_up, grad_down)


def solution(mesh):
    placed = (
        P(("rep", "ep"), None),
        P(("rep", "ep"), None),
        P(("rep", "ep"), None),
        P(("rep", "ep"), None),
        P("ep", None, None),
        P("ep", None, None),
        P("ep", None, None),
    )
    return jax.shard_map(
        per_device,
        mesh=mesh,
        in_specs=placed,
        out_specs=(
            P(("rep", "ep"), None),
            P(("rep", "ep"), None),
            P(("rep", "ep"), None),
            P("ep", "rep", None),
            P("ep", "rep", None),
            P("ep", "rep", None),
        ),
        check_vma=False,
    )
```

```python
import jax
import jax.numpy as jnp
from jax import lax
from jax.sharding import PartitionSpec as P

Z_CHIPS = 4
CORES = 2


def matmul(left, right, left_dim, right_dim):
    return lax.dot_general(
        left, right, (((left_dim,), (right_dim,)), ((), ())), preferred_element_type=jnp.float32
    )


def per_device(tokens, expert_ids, gate_weights, cotangent, w_gate, w_up, w_down):
    tok_rows, row_width = tokens.shape
    top_count = expert_ids.shape[1]
    expert_count = lax.axis_size("ep")
    rep_count = lax.axis_size("rep")
    x_chips = expert_count // (Z_CHIPS * CORES)
    capacity = top_count * tok_rows * 4 // (3 * expert_count)
    half_rows = Z_CHIPS * x_chips * capacity
    me = lax.axis_index("ep")
    my_rep = lax.axis_index("rep")
    my_core = me % CORES
    my_x = (me // CORES) % x_chips
    my_z = me // (CORES * x_chips)
    gate_matrix = w_gate[0]
    up_matrix = w_up[0]
    down_matrix = w_down[0]

    def place(z, x, core):
        return ((z % Z_CHIPS) * x_chips + x % x_chips) * CORES + core % CORES

    def shift(array, dz=0, dx=0, dc=0):
        pairs = [
            (place(z, x, c), place(z + dz, x + dx, c + dc))
            for z in range(Z_CHIPS)
            for x in range(x_chips)
            for c in range(CORES)
        ]
        return lax.ppermute(array, "ep", pairs)

    def gather_chips(block):
        lines = [block] + [shift(block, dz=k) for k in range(1, Z_CHIPS)]
        return [
            jnp.stack([b] + [shift(b, dx=k) for k in range(1, x_chips)]) for b in lines
        ]

    chosen = expert_ids[:, :, None] == jnp.arange(expert_count, dtype=jnp.int32)[None, None, :]
    weights = jnp.sum(jnp.where(chosen, gate_weights[:, :, None], 0.0), axis=1)
    named = jnp.any(chosen, axis=1)
    before = jnp.cumsum(named.astype(jnp.int32), axis=0) - 1
    slots = jnp.where(named, before, -1).astype(jnp.float32)
    table = lax.all_gather(jnp.stack([weights.T, slots.T]), "ep")

    token_lines = gather_chips(tokens)
    cot_lines = gather_chips(cotangent)

    zs = my_z - jnp.arange(Z_CHIPS)[:, None]
    xs = my_x - jnp.arange(x_chips)[None, :]

    def picks(source_core, expert):
        sources = place(zs, xs, source_core).reshape(-1)
        part = table[sources, :, expert].reshape(Z_CHIPS, x_chips, 2, tok_rows)
        pick = part[:, :, 1, None, :] == jnp.arange(capacity, dtype=jnp.float32)[:, None]
        return pick, jnp.sum(jnp.where(pick, part[:, :, 0, None, :], 0.0), axis=3)

    sibling = place(my_z, my_x, my_core + 1)
    pick_own, gate_own = picks(my_core, me)
    pick_far, gate_far = picks(my_core + 1, me)
    pick_sib, _ = picks(my_core, sibling)
    pick_both = jnp.concatenate([pick_own, pick_sib], axis=2).astype(jnp.bfloat16)
    gate = jnp.concatenate([gate_own.reshape(-1, 1), gate_far.reshape(-1, 1)], axis=0)

    def dispatch(lines):
        own, far = [], []
        for dz in range(Z_CHIPS):
            packed = jnp.einsum(
                "xct,xtd->xcd", pick_both[dz], lines[dz], preferred_element_type=jnp.float32
            ).astype(jnp.bfloat16)
            own.append(packed[:, :capacity].reshape(-1, row_width))
            far.append(shift(packed[:, capacity:].reshape(-1, row_width), dc=1))
        return jnp.concatenate(own + far, axis=0)

    def collect(rows):
        rows = rows.astype(jnp.bfloat16).reshape(CORES, Z_CHIPS, x_chips, capacity, row_width)
        total = None
        for dz in list(range(1, Z_CHIPS)) + [0]:
            both = jnp.concatenate([rows[0, dz], shift(rows[1, dz], dc=1)], axis=1)
            spread = jnp.einsum(
                "xct,xcd->xtd", pick_both[dz], both, preferred_element_type=jnp.float32
            ).astype(jnp.bfloat16)
            line = spread[0].astype(jnp.float32)
            for k in range(1, x_chips):
                line = line + shift(spread[k], dx=-k).astype(jnp.float32)
            if dz:
                line = shift(line.astype(jnp.bfloat16), dz=-dz).astype(jnp.float32)
            total = line if total is None else total + line
        return total.astype(jnp.bfloat16)

    def over_rep(left, right):
        part_width = left.shape[1] // rep_count

        def part(rep):
            cols = lax.dynamic_slice_in_dim(left, rep * part_width, part_width, axis=1)
            return matmul(cols, right, 0, 0).astype(jnp.bfloat16)

        received = []
        for k in range(1, rep_count):
            sent = part((my_rep + k) % rep_count)
            pairs = [(r, (r + k) % rep_count) for r in range(rep_count)]
            received.append(lax.ppermute(sent, "rep", pairs))
        total = part(my_rep).astype(jnp.float32)
        for other in received:
            total = total + other.astype(jnp.float32)
        return total[None]

    x_rows = dispatch(token_lines)
    gate_pre = matmul(x_rows, gate_matrix, 1, 0)
    up_pre = matmul(x_rows, up_matrix, 1, 0)
    sigmoid_val = jax.nn.sigmoid(gate_pre)
    silu_val = gate_pre * sigmoid_val
    act = silu_val * up_pre
    weighted = (gate * act).astype(jnp.bfloat16)
    mixed = collect(matmul(weighted, down_matrix, 1, 0))

    c_rows = dispatch(cot_lines)
    grad_down = over_rep(weighted, c_rows)
    back = matmul(c_rows, down_matrix, 1, 1)
    act_grad = gate * back
    gate_pre_grad = (
        act_grad * up_pre * sigmoid_val * (1.0 + gate_pre * (1.0 - sigmoid_val))
    ).astype(jnp.bfloat16)
    up_pre_grad = (act_grad * silu_val).astype(jnp.bfloat16)
    pair_grad = jnp.sum(act * back, axis=1)
    grad_gate = over_rep(x_rows, gate_pre_grad)
    grad_up = over_rep(x_rows, up_pre_grad)
    row_grad = matmul(gate_pre_grad, gate_matrix, 1, 1) + matmul(up_pre_grad, up_matrix, 1, 1)
    token_grad = collect(row_grad)

    pairs_own = pair_grad[:half_rows].reshape(Z_CHIPS, x_chips, capacity, 1)
    pairs_far = pair_grad[half_rows:].reshape(Z_CHIPS, x_chips, capacity, 1)
    pair_rows = jnp.stack(
        [
            jnp.sum(jnp.where(pick_own, pairs_own, 0.0), axis=2),
            jnp.sum(jnp.where(pick_far, pairs_far, 0.0), axis=2),
        ]
    )
    everyone = lax.all_gather(pair_rows, "ep")
    experts = jnp.arange(expert_count)
    from_z = experts // (CORES * x_chips)
    from_x = (experts // CORES) % x_chips
    pair_tok = everyone[
        experts, (experts + my_core) % CORES, (from_z - my_z) % Z_CHIPS, (from_x - my_x) % x_chips
    ]
    gate_grad = jnp.sum(jnp.where(chosen, pair_tok.T[:, None, :], 0.0), axis=2)
    return (mixed, token_grad, gate_grad, grad_gate, grad_up, grad_down)


def solution(mesh):
    placed = (
        P(("rep", "ep"), None),
        P(("rep", "ep"), None),
        P(("rep", "ep"), None),
        P(("rep", "ep"), None),
        P("ep", None, None),
        P("ep", None, None),
        P("ep", None, None),
    )
    return jax.shard_map(
        per_device,
        mesh=mesh,
        in_specs=placed,
        out_specs=(
            P(("rep", "ep"), None),
            P(("rep", "ep"), None),
            P(("rep", "ep"), None),
            P("ep", "rep", None),
            P("ep", "rep", None),
            P("ep", "rep", None),
        ),
        check_vma=False,
    )
```

```python
import jax
import jax.numpy as jnp
from jax import lax
from jax.sharding import PartitionSpec as P

Z_CHIPS = 4
CORES = 2


def matmul(left, right, left_dim, right_dim):
    return lax.dot_general(
        left, right, (((left_dim,), (right_dim,)), ((), ())), preferred_element_type=jnp.float32
    )


def per_device(tokens, expert_ids, gate_weights, cotangent, w_gate, w_up, w_down):
    tok_rows, row_width = tokens.shape
    top_count = expert_ids.shape[1]
    expert_count = lax.axis_size("ep")
    rep_count = lax.axis_size("rep")
    x_chips = expert_count // (Z_CHIPS * CORES)
    capacity = top_count * tok_rows * 4 // (3 * expert_count)
    half_rows = Z_CHIPS * x_chips * capacity
    me = lax.axis_index("ep")
    my_rep = lax.axis_index("rep")
    my_core = me % CORES
    my_x = (me // CORES) % x_chips
    my_z = me // (CORES * x_chips)
    gate_matrix = w_gate[0]
    up_matrix = w_up[0]
    down_matrix = w_down[0]

    def place(z, x, core):
        return ((z % Z_CHIPS) * x_chips + x % x_chips) * CORES + core % CORES

    def shift(array, dz=0, dx=0, dc=0):
        pairs = [
            (place(z, x, c), place(z + dz, x + dx, c + dc))
            for z in range(Z_CHIPS)
            for x in range(x_chips)
            for c in range(CORES)
        ]
        return lax.ppermute(array, "ep", pairs)

    def along(block, axis, count):
        return [block] + [shift(block, **{axis: k}) for k in range(1, count)]

    together = lax.optimization_barrier

    chosen = expert_ids[:, :, None] == jnp.arange(expert_count, dtype=jnp.int32)[None, None, :]
    weights = jnp.sum(jnp.where(chosen, gate_weights[:, :, None], 0.0), axis=1)
    named = jnp.any(chosen, axis=1)
    before = jnp.cumsum(named.astype(jnp.int32), axis=0) - 1
    slots = jnp.where(named, before, -1).astype(jnp.float32)
    table = jnp.stack([weights.T, slots.T])
    table = jnp.stack(along(table, "dz", Z_CHIPS))
    table = jnp.stack(along(table, "dx", x_chips), axis=1)
    table = jnp.stack(along(table, "dc", CORES))

    token_z = along(tokens, "dz", Z_CHIPS)
    token_x = [along(token_z[0], "dx", x_chips)]
    token_z, token_x, cotangent = together((token_z, token_x, cotangent))
    token_x = token_x + [along(block, "dx", x_chips) for block in token_z[1:]]
    cot_z = along(cotangent, "dz", Z_CHIPS)
    cot_x = [along(cot_z[0], "dx", x_chips)]
    token_x, cot_z, cot_x, table = together((token_x, cot_z, cot_x, table))

    def picks(far, expert):
        part = lax.dynamic_index_in_dim(table[far], expert, axis=3, keepdims=False)
        pick = part[:, :, 1, None, :] == jnp.arange(capacity, dtype=jnp.float32)[:, None]
        return pick, jnp.sum(jnp.where(pick, part[:, :, 0, None, :], 0.0), axis=3)

    sibling = place(my_z, my_x, my_core + 1)
    pick_own, gate_own = picks(0, me)
    pick_far, gate_far = picks(1, me)
    pick_sib, _ = picks(0, sibling)
    pick_both = jnp.concatenate([pick_own, pick_sib], axis=2).astype(jnp.bfloat16)
    gate = jnp.concatenate([gate_own.reshape(-1, 1), gate_far.reshape(-1, 1)], axis=0)

    def dispatch(lines):
        own, far = [], []
        for dz in range(Z_CHIPS):
            packed = jnp.einsum(
                "xct,xtd->xcd", pick_both[dz], jnp.stack(lines[dz]), preferred_element_type=jnp.float32
            ).astype(jnp.bfloat16)
            own.append(packed[:, :capacity].reshape(-1, row_width))
            far.append(shift(packed[:, capacity:].reshape(-1, row_width), dc=1))
        return jnp.concatenate(own + far, axis=0)

    def collect_x(rows):
        rows = rows.reshape(CORES, Z_CHIPS, x_chips, capacity, row_width)
        lines = []
        for dz in range(Z_CHIPS):
            both = jnp.concatenate([rows[0, dz], shift(rows[1, dz], dc=1)], axis=1)
            spread = jnp.einsum(
                "xct,xcd->xtd", pick_both[dz], both, preferred_element_type=jnp.float32
            ).astype(jnp.bfloat16)
            line = spread[0].astype(jnp.float32)
            for k in range(1, x_chips):
                line = line + shift(spread[k], dx=-k).astype(jnp.float32)
            lines.append(line.astype(jnp.bfloat16))
        return lines

    def collect_z(lines):
        total = lines[0].astype(jnp.float32)
        for dz in range(1, Z_CHIPS):
            total = total + shift(lines[dz], dz=-dz).astype(jnp.float32)
        return total.astype(jnp.bfloat16)

    def rep_part(left, right, rep):
        part_width = left.shape[1] // rep_count
        cols = lax.dynamic_slice_in_dim(left, rep * part_width, part_width, axis=1)
        return matmul(cols, right, 0, 0).astype(jnp.bfloat16)

    def rep_others(left, right):
        received = []
        for k in range(1, rep_count):
            pairs = [(r, (r + k) % rep_count) for r in range(rep_count)]
            received.append(
                lax.ppermute(rep_part(left, right, (my_rep + k) % rep_count), "rep", pairs)
            )
        return received

    def rep_sum(left, right, received):
        total = rep_part(left, right, my_rep).astype(jnp.float32)
        for other in received:
            total = total + other.astype(jnp.float32)
        return total[None]

    cot_x = cot_x + [along(block, "dx", x_chips) for block in cot_z[1:]]
    x_rows = dispatch(token_x)
    gate_pre = matmul(x_rows, gate_matrix, 1, 0)
    up_pre = matmul(x_rows, up_matrix, 1, 0)
    sigmoid_val = jax.nn.sigmoid(gate_pre)
    silu_val = gate_pre * sigmoid_val
    act = silu_val * up_pre
    weighted = (gate * act).astype(jnp.bfloat16)
    out_rows = matmul(weighted, down_matrix, 1, 0).astype(jnp.bfloat16)
    cot_x, out_rows, x_rows, gate_pre, up_pre, weighted = together(
        (cot_x, out_rows, x_rows, gate_pre, up_pre, weighted)
    )

    mixed_lines = collect_x(out_rows)
    c_rows = dispatch(cot_x)
    others_down = rep_others(weighted, c_rows)
    back = matmul(c_rows, down_matrix, 1, 1)
    sigmoid_val = jax.nn.sigmoid(gate_pre)
    silu_val = gate_pre * sigmoid_val
    act_grad = gate * back
    gate_pre_grad = (
        act_grad * up_pre * sigmoid_val * (1.0 + gate_pre * (1.0 - sigmoid_val))
    ).astype(jnp.bfloat16)
    up_pre_grad = (act_grad * silu_val).astype(jnp.bfloat16)
    pair_grad = jnp.sum(silu_val * up_pre * back, axis=1)
    others_gate = rep_others(x_rows, gate_pre_grad)
    others_up = rep_others(x_rows, up_pre_grad)
    row_grad = (
        matmul(gate_pre_grad, gate_matrix, 1, 1) + matmul(up_pre_grad, up_matrix, 1, 1)
    ).astype(jnp.bfloat16)
    mixed_lines, row_grad, x_rows, c_rows, gate_pre_grad, up_pre_grad, weighted, pair_grad = together(
        (mixed_lines, row_grad, x_rows, c_rows, gate_pre_grad, up_pre_grad, weighted, pair_grad)
    )

    mixed = collect_z(mixed_lines)
    grad_lines = collect_x(row_grad)
    mixed, grad_lines = together((mixed, grad_lines))
    token_grad = collect_z(grad_lines)
    grad_down = rep_sum(weighted, c_rows, others_down)
    grad_gate = rep_sum(x_rows, gate_pre_grad, others_gate)
    grad_up = rep_sum(x_rows, up_pre_grad, others_up)

    pairs_own = pair_grad[:half_rows].reshape(Z_CHIPS, x_chips, capacity, 1)
    pairs_far = pair_grad[half_rows:].reshape(Z_CHIPS, x_chips, capacity, 1)
    pair_own = jnp.sum(jnp.where(pick_own, pairs_own, 0.0), axis=2)
    pair_far = jnp.sum(jnp.where(pick_far, pairs_far, 0.0), axis=2)
    pairs = jnp.stack([pair_own, shift(pair_far, dc=1)])
    pairs = jnp.stack([pairs[:, :, 0]] + [shift(pairs[:, :, k], dx=-k) for k in range(1, x_chips)])
    pairs = jnp.stack(
        [pairs[:, :, 0]] + [shift(pairs[:, :, k], dz=-k) for k in range(1, Z_CHIPS)]
    )
    owners = place(
        my_z + jnp.arange(Z_CHIPS)[:, None, None],
        my_x + jnp.arange(x_chips)[None, :, None],
        my_core + jnp.arange(CORES)[None, None, :],
    ).reshape(-1)
    pairs = pairs.reshape(expert_count, tok_rows)
    named_by = expert_ids[:, :, None] == owners[None, None, :]
    gate_grad = jnp.sum(jnp.where(named_by, pairs.T[:, None, :], 0.0), axis=2)
    return (mixed, token_grad, gate_grad, grad_gate, grad_up, grad_down)


def solution(mesh):
    placed = (
        P(("rep", "ep"), None),
        P(("rep", "ep"), None),
        P(("rep", "ep"), None),
        P(("rep", "ep"), None),
        P("ep", None, None),
        P("ep", None, None),
        P("ep", None, None),
    )
    return jax.shard_map(
        per_device,
        mesh=mesh,
        in_specs=placed,
        out_specs=(
            P(("rep", "ep"), None),
            P(("rep", "ep"), None),
            P(("rep", "ep"), None),
            P("ep", "rep", None),
            P("ep", "rep", None),
            P("ep", "rep", None),
        ),
        check_vma=False,
    )
```
